256 devices in a mesh: dp: 4 (over x), ctx: 64 (over y, z, core).
Axes of the slice: x: 4, y: 4, z: 8, core: 2. Of those that a mesh axis runs over, the one named last changes fastest.
Arguments:
- queries: bfloat16 [131072, 1024], P(('dp', 'ctx')), parts along dimension 0, may hold values from -6 to 6
- keys: bfloat16 [131072, 1024], P(('dp', 'ctx')), parts along dimension 0, may hold values from -6 to 6
- values: bfloat16 [131072, 1024], P(('dp', 'ctx')), parts along dimension 0, may hold values from -6 to 6
- clip_ids: int32 [131072], P('dp'), parts along dimension 0, may hold values from 0 to 18, never falling along the last dimension, each value on 1 to 3584 neighbouring positions
Outputs:
- attended: bfloat16 [131072, 1024], P(('dp', 'ctx')), parts along dimension 0
The draws below stay inside these ranges and needn't reach their ends.
There are 4 independent parts, one for each index of `dp`. The reference program is written for one: setup_inputs(seed, part) draws one part's arguments, and reference() takes and returns one part's arrays. A program takes and returns all parts, laid end to end along the dimension named above; each array names one. Nothing has to cross between parts.
Inputs may be any that keep to these rules, and one draw needn't show every extreme that they name: `clip_ids`: clip numbers never fall along the tokens; each clip holds 1 to 3584 tokens and one holds exactly 3584.
All inputs are finite; a program needn't handle non-finite values.
Results may differ from the reference program's by a relative error of at most 0.0059.
Values may be sent and summed in bfloat16 or wider, within the bound.
A program may use at most 128 MiB of HBM per device.

```python
import math
import jax
import jax.numpy as jnp
import numpy as np
from jax import lax

HEADS = 8
HEAD_DIM = 128
TOKENS = 32768
CLIP_MOST = 3584
FRAME = 256
CLIPS = 19


def draw_queries(key, part):
    key = jax.random.fold_in(key, 11)
    drawn = jnp.clip(jax.random.normal(key, (TOKENS, HEADS * HEAD_DIM), jnp.float32), -6.0, 6.0)
    return drawn.astype(jnp.bfloat16)


def draw_keys(key, part):
    key = jax.random.fold_in(key, 13)
    drawn = jnp.clip(jax.random.normal(key, (TOKENS, HEADS * HEAD_DIM), jnp.float32), -6.0, 6.0)
    return drawn.astype(jnp.bfloat16)


def steps_of(own_key, extent, split, smallest, largest):
    def one(axis_at, shards_of):
        heights = jax.random.uniform(jax.random.fold_in(jax.random.fold_in(own_key, 6), axis_at), (shards_of,), jnp.float32, smallest / len(split), largest / len(split))
        return jnp.repeat(jnp.exp(heights), extent[axis_at] // shards_of).reshape((-1,) + (1,) * (len(extent) - axis_at - 1))

    loudness = one(*split[0])
    for cut in split[1:]:
        loudness = loudness * one(*cut)
    return loudness


def length_profile(number_of, total, bound, skew):
    portions = [(1 << 20) // math.isqrt(grade ** skew) + 1 for grade in range(2, number_of + 1)]
    surplus, holding = total - bound - (number_of - 1), [1] * (number_of - 1)
    while surplus > 0:
        free = [i for i in range(number_of - 1) if holding[i] < bound]
        pool, left = sum([portions[i] for i in free]), surplus
        for i in free:
            addition = min(bound - holding[i], max(1, left * portions[i] // pool), surplus)
            holding[i] = holding[i] + addition
            surplus = surplus - addition
    return np.array([bound] + holding)


def ragged_sizes(own_key, number_of, total, reach, skew):
    if number_of == 2:
        one = jax.random.randint(own_key, (), max(1, total - reach), min(reach, total - 1) + 1)
        return jnp.stack([one, total - one])
    sizes = jnp.asarray(length_profile(number_of, total, reach, skew), jnp.int32)
    pairs = (number_of - 1) // 2
    giver, sink = sizes[1:1 + 2 * pairs:2], sizes[2:2 + 2 * pairs:2]
    slack = jnp.minimum(giver - 1, reach - sink)
    passed = jax.random.randint(jax.random.fold_in(own_key, 1), (pairs,), 0, 1 << 20) % (slack + 1)
    sizes = sizes.at[1:1 + 2 * pairs:2].set(giver - passed).at[2:2 + 2 * pairs:2].set(sink + passed)
    return sizes[jax.random.permutation(jax.random.fold_in(own_key, 2), number_of)]


def centred(key, shape, spread, reach, cuts=(), held_as=jnp.bfloat16):
    level = steps_of(key, shape, cuts, -0.22, 0.18) if cuts else 1.0
    drawn = jax.random.normal(key, shape, jnp.float32) * spread * level
    return jnp.minimum(jnp.maximum(drawn, -reach), reach).astype(held_as)


def setup_inputs(seed: int = 0, part: int = 0) -> dict:
    key_list = jax.random.split(jax.random.key(seed), 5)
    own_keys = jax.random.split(jax.random.fold_in(key_list[4], part), 5)
    queries = draw_queries(jax.random.fold_in(jax.random.fold_in(key_list[4], part), 71), part)
    keys = draw_keys(jax.random.fold_in(jax.random.fold_in(key_list[4], part), 71), part)
    values = centred(own_keys[2], (TOKENS, HEADS * HEAD_DIM), 1.0, 6.0, ((0, 64),))
    clip_ids = jnp.searchsorted(jnp.cumsum(ragged_sizes(own_keys[3], CLIPS, TOKENS, CLIP_MOST, 1)), jnp.arange(TOKENS), side="right").astype(jnp.int32)
    return dict(queries=queries, keys=keys, values=values, clip_ids=clip_ids)


def reference(queries, keys, values, clip_ids):
    head_count = queries.shape[1] // HEAD_DIM
    block_rows = min(512, TOKENS)
    window_rows = min(CLIP_MOST + block_rows, TOKENS)
    softmax_scale = 1.0 / math.sqrt(HEAD_DIM)

    def one_block(block_index):
        query_start = (block_index * block_rows).astype(jnp.int32)
        key_start = jnp.clip(query_start + block_rows - window_rows, 0, TOKENS - window_rows).astype(jnp.int32)
        query_rows = lax.dynamic_slice_in_dim(queries, query_start, block_rows, 0)
        key_rows = lax.dynamic_slice_in_dim(keys, key_start, window_rows, 0)
        value_rows = lax.dynamic_slice_in_dim(values, key_start, window_rows, 0)
        query_clip = lax.dynamic_slice_in_dim(clip_ids, query_start, block_rows, 0)
        key_clip = lax.dynamic_slice_in_dim(clip_ids, key_start, window_rows, 0)
        query_pos = query_start + jnp.arange(block_rows, dtype=jnp.int32)
        key_pos = key_start + jnp.arange(window_rows, dtype=jnp.int32)
        allowed = (key_clip[None, :] == query_clip[:, None]) & ((key_pos // FRAME)[None, :] <= (query_pos // FRAME)[:, None])
        query_heads = query_rows.reshape(block_rows, head_count, HEAD_DIM).astype(jnp.float32)
        key_heads = key_rows.reshape(window_rows, head_count, HEAD_DIM).astype(jnp.float32)
        value_heads = value_rows.reshape(window_rows, head_count, HEAD_DIM).astype(jnp.float32)
        scores = jnp.einsum('qhd,khd->qhk', query_heads, key_heads) * softmax_scale
        mask_heads = allowed[:, None, :]
        row_max = lax.optimization_barrier(jnp.max(jnp.where(mask_heads, scores, -1e+30), axis=-1))
        weights = jnp.where(mask_heads, jnp.exp(scores - row_max[..., None]), 0.0)
        total = lax.optimization_barrier(jnp.sum(weights, axis=-1))
        rounded = weights.astype(jnp.bfloat16).astype(jnp.float32)
        mixed = jnp.einsum('qhk,khd->qhd', rounded, value_heads) / total[..., None]
        return mixed.astype(jnp.bfloat16)
    blocks = lax.map(one_block, jnp.arange(TOKENS // block_rows, dtype=jnp.int32))
    return blocks.reshape(TOKENS, head_count * HEAD_DIM)
```

```python
import functools
import math

import jax
import jax.numpy as jnp
from jax import lax
from jax.experimental import pallas as pl
from jax.experimental.pallas import tpu as pltpu
from jax.sharding import PartitionSpec as P

HEAD_DIM = 128
FRAME = 256
MESH = pl.DeviceIdType.MESH
F32 = jnp.float32
BF16 = jnp.bfloat16

CHIP = 1024
HALF = 512
LANE_HEADS = 4
WIDTH = LANE_HEADS * HEAD_DIM
T = 128
K = CHIP // T
HOPS = 3
PENALTY = 16384.0
SCALE = math.log2(math.e) / math.sqrt(HEAD_DIM)


def nt_dot(a, b):
    return lax.dot_general(a, b, (((1,), (1,)), ((), ())), preferred_element_type=F32)


def attend(q, qa, key_of, value_of, key_mask, lse_in, out_in):
    rows = q.shape[0]
    lane = lax.broadcasted_iota(jnp.int32, (rows, 128), 1)
    stats = jnp.zeros((rows, 128), F32)
    outs = []
    for h in range(LANE_HEADS):
        cols = slice(h * HEAD_DIM, (h + 1) * HEAD_DIM)
        scores = nt_dot(
            jnp.concatenate([q[:, cols], qa], axis=1),
            jnp.concatenate([key_of(cols), key_mask], axis=1),
        )
        top = jnp.max(scores, axis=1, keepdims=True) * SCALE
        if lse_in is not None:
            before = lse_in[:, h : h + 1]
            top = jnp.maximum(top, before)
        weights = jnp.exp2(scores * SCALE - top).astype(BF16)
        values = value_of(cols)
        both = jnp.dot(
            weights,
            jnp.concatenate([values, jnp.ones_like(values)], axis=1),
            preferred_element_type=F32,
        )
        mixed, total = both[:, :HEAD_DIM], both[:, HEAD_DIM:]
        if lse_in is not None:
            keep = jnp.exp2(before - top)
            mixed = mixed + out_in[:, cols].astype(F32) * keep
            total = total + keep
        outs.append((mixed / total).astype(BF16))
        stats = jnp.where(lane == h, top + jnp.log2(total), stats)
    return outs, stats


def kernel(
    q_ref, k_ref, v_ref, clip_ref, out_ref,
    qb, kb, vb, kl, vl, qa, ka, kla, oin, oout, lin, lout, cw,
    load_sem, clip_sem, sib_send, sib_recv, left_send, left_recv,
    q_send, q_recv, o_send, o_recv, l_send, l_recv, out_sem, out_send, out_recv,
):
    size = lax.axis_size("ctx")
    chips = size // 2
    me = lax.axis_index("ctx")
    core = lax.rem(me, 2)
    chip = me // 2
    sib = chip * 2 + (1 - core)
    prev = lax.rem(me + size - 2, size)
    nxt = lax.rem(me + 2, size)

    def remote(src, dst, send, recv, to):
        return pltpu.make_async_remote_copy(
            src_ref=src, dst_ref=dst, send_sem=send, recv_sem=recv,
            device_id={"ctx": to}, device_id_type=MESH,
        )

    mine = pl.ds(pl.multiple_of(core * HALF, HALF), HALF)
    theirs = pl.ds(pl.multiple_of((1 - core) * HALF, HALF), HALF)
    whole = pl.ds(0, HALF)

    loads = [
        pltpu.make_async_copy(src.at[whole, mine], dst, load_sem.at[i])
        for i, (src, dst) in enumerate(
            [(q_ref, qb.at[0, mine]), (k_ref, kb.at[mine]), (v_ref, vb.at[mine])]
        )
    ]
    for copy in loads:
        copy.start()
    clips = []
    for i in range(HOPS + 2):
        row = pl.multiple_of(lax.rem(chip + chips - 1 + i, chips) * 8, 8)
        clips.append(
            pltpu.make_async_copy(clip_ref.at[pl.ds(row, 8)], cw.at[pl.ds(8 * i, 8)], clip_sem.at[i])
        )
    for copy in clips:
        copy.start()

    barrier = pltpu.get_barrier_semaphore()
    for to in (sib, prev, nxt):
        pl.semaphore_signal(barrier, inc=1, device_id={"ctx": to}, device_id_type=MESH)
    pl.semaphore_wait(barrier, 3)

    swaps = [
        remote(src.at[whole, theirs], dst, sib_send.at[i], sib_recv.at[i], sib)
        for i, (src, dst) in enumerate(
            [(q_ref, qb.at[0, mine]), (k_ref, kb.at[mine]), (v_ref, vb.at[mine])]
        )
    ]
    for copy in swaps:
        copy.start()

    def rows_of(k):
        return pl.ds(pl.multiple_of(lax.rem(k + K // 2, K) * T, T), T)

    def send_q(d, k):
        r = rows_of(k)
        return remote(qb.at[d - 1, r], qb.at[d, r], q_send.at[d - 1, k], q_recv.at[d - 1, k], prev)

    def send_o(d, k):
        r = rows_of(k)
        return remote(oout.at[d, r], oin.at[d - 1, r], o_send.at[d - 1, k], o_recv.at[d - 1, k], nxt)

    def send_l(d, k):
        return remote(lout.at[d, k], lin.at[d - 1, k], l_send.at[d - 1, k], l_recv.at[d - 1, k], nxt)

    loads[0].wait()
    swaps[0].wait_recv()
    send_q(1, 0).start()

    for i in (1, 2):
        loads[i].wait()
        swaps[i].wait_recv()
    late = pl.ds(HALF, HALF)
    lefts = [
        remote(kb.at[late], kl, left_send.at[0], left_recv.at[0], nxt),
        remote(vb.at[late], vl, left_send.at[1], left_recv.at[1], nxt),
    ]
    for copy in lefts:
        copy.start()

    for copy in clips:
        copy.wait()
    lane = lax.broadcasted_iota(jnp.int32, (128, 128), 1)

    def clip_columns(row):
        wide = jnp.broadcast_to(cw[pl.ds(row, 1), :].astype(F32), (128, 128))
        return wide.T.astype(jnp.int32)

    @pl.loop(0, 4)
    def _(i):
        same = clip_columns(4 + i) == lane
        kla[pl.ds(pl.multiple_of(i * 128, 128), 128), :] = jnp.where(
            same | (lane >= 32), 0.0, -PENALTY
        ).astype(BF16)

    @pl.loop(0, 8)
    def _(i):
        same = clip_columns(8 + i) == lane
        frame = i // (FRAME // 128)
        r = pl.ds(pl.multiple_of(i * 128, 128), 128)
        later = (lane >= 32) & (frame > lane - 32)
        ka[r, :] = jnp.where((~same & (lane < 32)) | later, -PENALTY, 0.0).astype(BF16)
        qa[0, r, :] = jnp.where(same | (lane == 32 + frame), 1.0, 0.0).astype(BF16)

    @pl.loop(0, 8 * HOPS)
    def _(i):
        same = clip_columns(16 + i) == lane
        r = pl.ds(pl.multiple_of(lax.rem(i, 8) * 128, 128), 128)
        qa[1 + i // 8, r, :] = jnp.where(same, 1.0, 0.0).astype(BF16)

    oin[HOPS] = jnp.zeros((CHIP, WIDTH), BF16)
    lin[HOPS] = jnp.full((K, 8, T), -1e30, F32)

    def store_stats(ref, d, k, stats):
        ref[d, k] = stats.T[:8, :]

    @pl.loop(0, K + 2 * HOPS)
    def _(j):
        @pl.when((j >= 1) & (j < K))
        def _():
            send_q(1, j).start()

        for hop in range(1, HOPS):
            @pl.when((j >= hop) & (j < K + hop))
            def _(hop=hop):
                send_q(hop, j - hop).wait_recv()
                send_q(hop + 1, j - hop).start()

        @pl.when((j >= HOPS) & (j < K + HOPS))
        def _():
            k = j - HOPS
            send_q(HOPS, k).wait_recv()

            @pl.when(k == K // 2)
            def _():
                for copy in lefts:
                    copy.wait_recv()

            @pl.when(k >= K // 2)
            def _():
                r = rows_of(k)
                outs, stats = attend(
                    qb[HOPS, r, :], qa[HOPS, r, :],
                    lambda cols: kl[:, cols], lambda cols: vl[:, cols], kla[...], None, None,
                )
                oin[HOPS, r, :] = jnp.concatenate(outs, axis=1)
                store_stats(lin, HOPS, k, stats)

        @pl.loop(0, HOPS + 1)
        def _(back):
            d = HOPS - back
            k = j - HOPS - back

            @pl.when((k >= 0) & (k < K))
            def _():
                @pl.when(d < HOPS)
                def _():
                    send_o(d + 1, k).wait_recv()
                    send_l(d + 1, k).wait_recv()

                r = rows_of(k)
                lse = jnp.concatenate([lin[d, k], jnp.zeros((120, T), F32)], axis=0).T
                outs, stats = attend(
                    qb[d, r, :], qa[d, r, :],
                    lambda cols: kb[:, cols], lambda cols: vb[:, cols], ka[...], lse, oin[d, r, :],
                )
                oout[d, r, :] = jnp.concatenate(outs, axis=1)
                store_stats(lout, d, k, stats)

                @pl.when(d > 0)
                def _():
                    send_o(d, k).start()
                    send_l(d, k).start()

    here = pltpu.make_async_copy(oout.at[0, mine], out_ref.at[whole, mine], out_sem)
    there = remote(oout.at[0, theirs], out_ref.at[whole, mine], out_send, out_recv, sib)
    there.start()
    here.start()

    for copy in swaps + lefts:
        copy.wait_send()

    @pl.loop(0, K)
    def _(k):
        for d in range(1, HOPS + 1):
            send_q(d, k).wait_send()
            send_o(d, k).wait_send()
            send_l(d, k).wait_send()

    here.wait()
    there.wait()


def per_device(queries, keys, values, clip_ids):
    tokens, width = queries.shape
    anywhere = pl.BlockSpec(memory_space=pl.ANY)
    dma = pltpu.SemaphoreType.DMA
    return pl.pallas_call(
        kernel,
        out_shape=jax.ShapeDtypeStruct((tokens, width), BF16),
        in_specs=[anywhere] * 4,
        out_specs=anywhere,
        scratch_shapes=[
            pltpu.VMEM((HOPS + 1, CHIP, WIDTH), BF16),
            pltpu.VMEM((CHIP, WIDTH), BF16),
            pltpu.VMEM((CHIP, WIDTH), BF16),
            pltpu.VMEM((HALF, WIDTH), BF16),
            pltpu.VMEM((HALF, WIDTH), BF16),
            pltpu.VMEM((HOPS + 1, CHIP, 128), BF16),
            pltpu.VMEM((CHIP, 128), BF16),
            pltpu.VMEM((HALF, 128), BF16),
            pltpu.VMEM((HOPS + 1, CHIP, WIDTH), BF16),
            pltpu.VMEM((HOPS + 1, CHIP, WIDTH), BF16),
            pltpu.VMEM((HOPS + 1, K, 8, T), F32),
            pltpu.VMEM((HOPS + 1, K, 8, T), F32),
            pltpu.VMEM((8 * (HOPS + 2), 128), jnp.int32),
            dma((3,)), dma((HOPS + 2,)), dma((3,)), dma((3,)), dma((2,)), dma((2,)),
            dma((HOPS, K)), dma((HOPS, K)), dma((HOPS, K)), dma((HOPS, K)),
            dma((HOPS, K)), dma((HOPS, K)),
            dma, dma, dma,
        ],
        compiler_params=pltpu.CompilerParams(
            collective_id=0, has_side_effects=True, vmem_limit_bytes=48 << 20
        ),
        name="chain_attention",
    )(queries, keys, values, clip_ids.reshape(-1, 128))


def solution(mesh):
    placed = (P(("dp", "ctx"), None), P(("dp", "ctx"), None), P(("dp", "ctx"), None), P("dp"))
    return jax.shard_map(
        per_device, mesh=mesh, in_specs=placed, out_specs=P(("dp", "ctx"), None), check_vma=False
    )
```

```python
import functools
import math

import jax
import jax.numpy as jnp
from jax import lax
from jax.experimental import pallas as pl
from jax.experimental.pallas import tpu as pltpu
from jax.sharding import PartitionSpec as P

HEAD_DIM = 128
FRAME = 256
MESH = pl.DeviceIdType.MESH
F32 = jnp.float32
BF16 = jnp.bfloat16

CHIP = 1024
HALF = 512
LANE_HEADS = 4
WIDTH = LANE_HEADS * HEAD_DIM
T = 128
K = CHIP // T
HOPS = 3
PENALTY = 16384.0
SCALE = math.log2(math.e) / math.sqrt(HEAD_DIM)


def attend(rows_of_head, keys_of_head, values_of_head, store):
    heads = range(LANE_HEADS)
    scores = [
        lax.dot_general(
            rows_of_head(h), keys_of_head(h), (((1,), (1,)), ((), ())), preferred_element_type=F32
        )
        for h in heads
    ]
    tops = [jnp.max(s, axis=1, keepdims=True) * SCALE for s in scores]
    weights = [jnp.exp2(s * SCALE - top).astype(BF16) for s, top in zip(scores, tops)]
    stats = 0.0
    for h in heads:
        both = jnp.dot(weights[h], values_of_head(h), preferred_element_type=F32)
        mixed, total = both[:, :HEAD_DIM], both[:, HEAD_DIM:]
        store(h, mixed / total)
        lane = lax.broadcasted_iota(jnp.int32, total.shape, 1)
        stats = jnp.where(lane == h, tops[h] + jnp.log2(total), stats)
    return stats


def join(part, part_lse, other, other_lse):
    top = jnp.maximum(part_lse, other_lse)
    a = jnp.exp2(part_lse - top)
    b = jnp.exp2(other_lse - top)
    total = a + b
    a = a / total
    b = b / total
    mixed = []
    for h in range(LANE_HEADS):
        cols = slice(h * HEAD_DIM, (h + 1) * HEAD_DIM)
        mixed.append(part[:, cols] * a[:, h : h + 1] + other[:, cols].astype(F32) * b[:, h : h + 1])
    return jnp.concatenate(mixed, axis=1), top + jnp.log2(total)


def kernel(
    q_ref, k_ref, v_ref, clip_ref, out_ref,
    qb, kb, vb, kl, vl, qa, stage, part, part_lse, hpart, hlse, extra, oin, oout, lin, lout, cw,
    load_sem, clip_sem, sib_send, sib_recv, left_send, left_recv,
    q_send, q_recv, o_send, o_recv, l_send, l_recv, out_sem, out_send, out_recv,
):
    size = lax.axis_size("ctx")
    chips = size // 2
    me = lax.axis_index("ctx")
    core = lax.rem(me, 2)
    chip = me // 2
    sib = chip * 2 + (1 - core)
    prev = lax.rem(me + size - 2, size)
    nxt = lax.rem(me + 2, size)
    prev_sib = prev + 1 - 2 * core
    nxt_sib = nxt + 1 - 2 * core

    def remote(src, dst, send, recv, to):
        return pltpu.make_async_remote_copy(
            src_ref=src, dst_ref=dst, send_sem=send, recv_sem=recv,
            device_id={"ctx": to}, device_id_type=MESH,
        )

    mine = pl.ds(pl.multiple_of(core * HALF, HALF), HALF)
    theirs = pl.ds(pl.multiple_of((1 - core) * HALF, HALF), HALF)
    whole = pl.ds(0, HALF)
    front = pl.ds(0, HEAD_DIM)

    def moves(base):
        pairs = [(q_ref.at[whole, pl.ds(pl.multiple_of(base, HALF), HALF)], qb.at[0, mine])]
        for src, dst in ((k_ref, kb), (v_ref, vb)):
            for h in range(LANE_HEADS):
                cols = pl.ds(pl.multiple_of(base + h * HEAD_DIM, HEAD_DIM), HEAD_DIM)
                pairs.append((src.at[whole, cols], dst.at[h, mine, front]))
        return pairs

    loads = [
        pltpu.make_async_copy(src, dst, load_sem.at[i])
        for i, (src, dst) in enumerate(moves(core * HALF))
    ]
    for copy in loads:
        copy.start()
    clips = []
    for i in range(HOPS + 2):
        row = pl.multiple_of(lax.rem(chip + chips - 1 + i, chips) * 8, 8)
        clips.append(
            pltpu.make_async_copy(clip_ref.at[pl.ds(row, 8)], cw.at[pl.ds(8 * i, 8)], clip_sem.at[i])
        )
    for copy in clips:
        copy.start()
    lin[...] = jnp.zeros(lin.shape, F32)

    barrier = pltpu.get_barrier_semaphore()
    for to in (sib, prev, nxt, prev_sib, nxt_sib):
        pl.semaphore_signal(barrier, inc=1, device_id={"ctx": to}, device_id_type=MESH)

    for copy in clips:
        copy.wait()
    lane = lax.broadcasted_iota(jnp.int32, (128, 128), 1)

    def clip_columns(row):
        wide = jnp.broadcast_to(cw[pl.ds(row, 1), :].astype(F32), (128, 128))
        return wide.T.astype(jnp.int32)

    ones = jnp.ones((128, HEAD_DIM), BF16)

    def prepare_own():
        @pl.loop(0, 8)
        def _(i):
            same = clip_columns(8 + i) == lane
            r = pl.ds(pl.multiple_of(i * 128, 128), 128)
            mask = jnp.where(same | (lane >= 32), 0.0, -PENALTY).astype(BF16)
            for h in range(LANE_HEADS):
                kb[h, r, HEAD_DIM:] = mask
                vb[h, r, HEAD_DIM:] = ones
            qa[0, r, :] = jnp.where(same, 1.0, 0.0).astype(BF16)

    def prepare_left():
        @pl.loop(0, 4)
        def _(i):
            same = clip_columns(4 + i) == lane
            r = pl.ds(pl.multiple_of(i * 128, 128), 128)
            mask = jnp.where(same | (lane >= 32), 0.0, -PENALTY).astype(BF16)
            for h in range(LANE_HEADS):
                kl[h, r, HEAD_DIM:] = mask
                vl[h, r, HEAD_DIM:] = ones

    def prepare_visitors(start):
        @pl.loop(0, 12)
        def _(i):
            i = start + i
            same = clip_columns(16 + i) == lane
            r = pl.ds(pl.multiple_of(lax.rem(i, 8) * 128, 128), 128)
            qa[1 + i // 8, r, :] = jnp.where(same, 1.0, 0.0).astype(BF16)

    prepare_own()
    prepare_visitors(0)
    prepare_visitors(12)
    prepare_left()
    pl.semaphore_wait(barrier, 5)

    swaps = [
        remote(src, dst, sib_send.at[i], sib_recv.at[i], sib)
        for i, (src, dst) in enumerate(moves((1 - core) * HALF))
    ]

    def rows_of(k):
        return pl.ds(pl.multiple_of(lax.rem(k + K // 2, K) * T, T), T)

    def send_q(d, k):
        r = rows_of(k)
        return remote(qb.at[d - 1, r], qb.at[d, r], q_send.at[d - 1], q_recv.at[d - 1, k], prev)

    def send_own(k, lane, to):
        rows = pl.ds(pl.multiple_of(lax.rem(k, K // 2) * T, T), T)
        cols = pl.ds(lane * WIDTH, WIDTH)
        return remote(q_ref.at[rows, cols], qb.at[1, rows_of(k)], q_send.at[0], q_recv.at[0, k], to)

    def start_own(k):
        @pl.when(core == 1 - k // (K // 2))
        def _():
            for lane in range(2):
                send_own(k, lane, 2 * (prev // 2) + lane).start()

    def send_o(d, k):
        r = rows_of(k)
        return remote(oout.at[d, r], oin.at[d - 1, r], o_send.at[d - 1], o_recv.at[d - 1, k], nxt)

    def send_l(d, k):
        rows = pl.ds(0, LANE_HEADS)
        return remote(
            lout.at[d, k, rows], lin.at[d - 1, k, rows], l_send.at[d - 1], l_recv.at[d - 1, k], nxt
        )

    def left_copy(lane, i):
        src, dst = ((k_ref, kl), (v_ref, vl))[i // LANE_HEADS]
        h = i % LANE_HEADS
        cols = pl.ds(lane * WIDTH + h * HEAD_DIM, HEAD_DIM)
        return remote(
            src.at[whole, cols], dst.at[h, :, front], left_send.at[lane, i], left_recv.at[i],
            2 * (nxt // 2) + lane,
        )

    start_own(0)

    @pl.when(core == 1)
    def _():
        for i in range(2 * LANE_HEADS):
            for lane in range(2):
                left_copy(lane, i).start()

    for copy in swaps:
        copy.start()

    stage[...] = jnp.zeros(stage.shape, BF16)
    blank = jnp.zeros((128 - T, 128), F32)

    def own_block(b):
        rows, seen = pl.ds(b * FRAME, FRAME), pl.ds(0, (b + 1) * FRAME)

        def queries(h):
            return jnp.concatenate(
                [qb[0, rows, h * HEAD_DIM : (h + 1) * HEAD_DIM], qa[0, rows, :]], axis=1
            )

        def store(h, value):
            hpart[rows, h * HEAD_DIM : (h + 1) * HEAD_DIM] = value

        hlse[rows, :] = attend(queries, lambda h: kb[h, seen, :], lambda h: vb[h, seen, :], store)

    def hand_on(d, k, mixed, lse):
        oout[d, rows_of(k), :] = mixed.astype(BF16)
        if d > 0:
            send_o(d, k).start()
            lout[d, k] = lse.T[:8, :]
            send_l(d, k).start()

    def piece_out(k):
        rows = pl.ds(pl.multiple_of(lax.rem(k, K // 2) * T, T), T)
        return oout.at[0, rows_of(k)], out_ref.at[rows, mine]

    def give_local(k):
        src, dst = piece_out(k)
        return pltpu.make_async_copy(src, dst, out_sem.at[lax.rem(k, K // 2)])

    def give_remote(k):
        src, dst = piece_out(k)
        i = lax.rem(k, K // 2)
        return remote(src, dst, out_send.at[i], out_recv.at[i], sib)

    @pl.loop(0, K + 2 * HOPS)
    def _(j):
        for d in range(HOPS, 0, -1):
            k = j - HOPS - (HOPS - d)
            here = slice((d - 1) * T, d * T)

            @pl.when((k >= 0) & (k < K))
            def _(d=d, k=k, here=here):
                if d == HOPS:
                    send_q(HOPS, k).wait_recv()
                r = rows_of(k)
                for h in range(LANE_HEADS):
                    stage[h, here, :HEAD_DIM] = qb[d, r, h * HEAD_DIM : (h + 1) * HEAD_DIM]
                    stage[h, here, HEAD_DIM:] = qa[d, r, :]

        @pl.when((j >= HOPS) & (j < K + 2 * HOPS - 1))
        def _():
            def store(h, value):
                part[:, h * HEAD_DIM : (h + 1) * HEAD_DIM] = value

            part_lse[...] = attend(
                lambda h: stage[h], lambda h: kb[h], lambda h: vb[h], store
            )

        far = slice((HOPS - 1) * T, HOPS * T)

        @pl.when((j >= HOPS + K // 2) & (j < HOPS + K))
        def _():
            @pl.when(j == HOPS + K // 2)
            def _():
                for i in range(2 * LANE_HEADS):
                    left_copy(0, i).wait_recv()

            def store(h, value):
                extra[:, h * HEAD_DIM : (h + 1) * HEAD_DIM] = value

            lse = attend(lambda h: stage[h, far, :], lambda h: kl[h], lambda h: vl[h], store)
            mixed, lse = join(part[far, :], part_lse[far, :], extra[...], lse)
            part[far, :] = mixed
            part_lse[far, :] = lse

        @pl.when((j >= HOPS) & (j < HOPS + K))
        def _():
            hand_on(HOPS, j - HOPS, part[far, :], part_lse[far, :])

        for hop in range(HOPS - 1, 0, -1):
            @pl.when((j >= hop) & (j < K + hop))
            def _(hop=hop):
                send_q(hop, j - hop).wait_recv()
                send_q(hop + 1, j - hop).start()

        @pl.when((j >= 1) & (j < K))
        def _():
            start_own(j)

        for b in range(CHIP // FRAME):
            @pl.when(j == b)
            def _(b=b):
                if b == 0:
                    for load, swap in zip(loads, swaps):
                        load.wait()
                        swap.wait_recv()
                own_block(b)

        for d in range(HOPS - 1, -1, -1):
            k = j - HOPS - (HOPS - d)

            @pl.when((k >= 0) & (k < K))
            def _(d=d, k=k):
                send_l(d + 1, k).wait_recv()
                send_o(d + 1, k).wait_recv()
                r = rows_of(k)
                arrived = jnp.concatenate([lin[d, k], jnp.zeros((120, 128), F32)], axis=0).T[:T, :]
                if d == 0:
                    mixed, lse = join(hpart[r, :], hlse[r, :], oin[d, r, :], arrived)
                else:
                    here = slice((d - 1) * T, d * T)
                    mixed, lse = join(part[here, :], part_lse[here, :], oin[d, r, :], arrived)
                hand_on(d, k, mixed, lse)
                if d == 0:
                    for owner in range(2):
                        @pl.when((k // (K // 2) == 1 - owner) & (core == owner))
                        def _():
                            give_local(k).start()

                        @pl.when((k // (K // 2) == 1 - owner) & (core != owner))
                        def _():
                            give_remote(k).start()

    for copy in swaps:
        copy.wait_send()

    @pl.when(core == 1)
    def _():
        for i in range(2 * LANE_HEADS):
            for lane in range(2):
                left_copy(lane, i).wait_send()

    for d in range(1, HOPS + 1):
        remote(qb.at[d - 1], qb.at[d], q_send.at[d - 1], q_recv.at[d - 1, 0], prev).wait_send()
        remote(oout.at[d], oin.at[d - 1], o_send.at[d - 1], o_recv.at[d - 1, 0], nxt).wait_send()
        rows = pl.ds(0, LANE_HEADS)
        remote(
            lout.at[d, :, rows], lin.at[d - 1, :, rows], l_send.at[d - 1], l_recv.at[d - 1, 0], nxt
        ).wait_send()

    @pl.loop(0, K // 2)
    def _(k):
        give_local(k).wait()
        give_remote(k).wait()


def per_device(queries, keys, values, clip_ids):
    tokens, width = queries.shape
    anywhere = pl.BlockSpec(memory_space=pl.ANY)
    dma = pltpu.SemaphoreType.DMA
    stacked = HOPS * T
    moved = 1 + 2 * LANE_HEADS
    return pl.pallas_call(
        kernel,
        out_shape=jax.ShapeDtypeStruct((tokens, width), BF16),
        in_specs=[anywhere] * 4,
        out_specs=anywhere,
        scratch_shapes=[
            pltpu.VMEM((HOPS + 1, CHIP, WIDTH), BF16),
            pltpu.VMEM((LANE_HEADS, CHIP, 2 * HEAD_DIM), BF16),
            pltpu.VMEM((LANE_HEADS, CHIP, 2 * HEAD_DIM), BF16),
            pltpu.VMEM((LANE_HEADS, HALF, 2 * HEAD_DIM), BF16),
            pltpu.VMEM((LANE_HEADS, HALF, 2 * HEAD_DIM), BF16),
            pltpu.VMEM((HOPS + 1, CHIP, 128), BF16),
            pltpu.VMEM((LANE_HEADS, stacked, 2 * HEAD_DIM), BF16),
            pltpu.VMEM((stacked, WIDTH), F32),
            pltpu.VMEM((stacked, 128), F32),
            pltpu.VMEM((CHIP, WIDTH), F32),
            pltpu.VMEM((CHIP, 128), F32),
            pltpu.VMEM((T, WIDTH), F32),
            pltpu.VMEM((HOPS, CHIP, WIDTH), BF16),
            pltpu.VMEM((HOPS + 1, CHIP, WIDTH), BF16),
            pltpu.VMEM((HOPS, K, 8, 128), F32),
            pltpu.VMEM((HOPS + 1, K, 8, 128), F32),
            pltpu.VMEM((8 * (HOPS + 2), 128), jnp.int32),
            dma((moved,)), dma((HOPS + 2,)), dma((moved,)), dma((moved,)),
            dma((2, moved - 1)), dma((moved - 1,)),
            dma((HOPS,)), dma((HOPS, K)), dma((HOPS,)), dma((HOPS, K)), dma((HOPS,)), dma((HOPS, K)),
            dma((K // 2,)), dma((K // 2,)), dma((K // 2,)),
        ],
        compiler_params=pltpu.CompilerParams(
            collective_id=0, has_side_effects=True, vmem_limit_bytes=62 << 20
        ),
        name="chain_attention",
    )(queries, keys, values, clip_ids.reshape(-1, 128))


def solution(mesh):
    placed = (P(("dp", "ctx"), None), P(("dp", "ctx"), None), P(("dp", "ctx"), None), P("dp"))
    return jax.shard_map(
        per_device, mesh=mesh, in_specs=placed, out_specs=P(("dp", "ctx"), None), check_vma=False
    )
```

```python
import functools
import math

import jax
import jax.numpy as jnp
from jax import lax
from jax.experimental import pallas as pl
from jax.experimental.pallas import tpu as pltpu
from jax.sharding import PartitionSpec as P

HEAD_DIM = 128
FRAME = 256
MESH = pl.DeviceIdType.MESH
F32 = jnp.float32
BF16 = jnp.bfloat16

CHIP = 1024
HALF = 512
LANE_HEADS = 4
WIDTH = LANE_HEADS * HEAD_DIM
T = 128
K = CHIP // T
REST = T
HOPS = 3
PENALTY = 16384.0
SCALE = math.log2(math.e) / math.sqrt(HEAD_DIM)


def attend(rows_of_head, keys_of_head, values_of_head, store):
    heads = range(LANE_HEADS)
    scores = [
        lax.dot_general(
            rows_of_head(h), keys_of_head(h), (((1,), (1,)), ((), ())), preferred_element_type=F32
        )
        for h in heads
    ]
    tops = [jnp.max(s, axis=1, keepdims=True) * SCALE for s in scores]
    weights = [jnp.exp2(s * SCALE - top).astype(BF16) for s, top in zip(scores, tops)]
    stats = 0.0
    for h in heads:
        both = jnp.dot(weights[h], values_of_head(h), preferred_element_type=F32)
        mixed, total = both[:, :HEAD_DIM], both[:, HEAD_DIM:]
        store(h, mixed / total)
        lane = lax.broadcasted_iota(jnp.int32, total.shape, 1)
        stats = jnp.where(lane == h, tops[h] + jnp.log2(total), stats)
    return stats


def join(part, part_lse, other, other_lse):
    top = jnp.maximum(part_lse, other_lse)
    a = jnp.exp2(part_lse - top)
    b = jnp.exp2(other_lse - top)
    total = a + b
    a = a / total
    b = b / total
    mixed = []
    for h in range(LANE_HEADS):
        cols = slice(h * HEAD_DIM, (h + 1) * HEAD_DIM)
        mixed.append(part[:, cols] * a[:, h : h + 1] + other[:, cols].astype(F32) * b[:, h : h + 1])
    return jnp.concatenate(mixed, axis=1), top + jnp.log2(total)


def kernel(
    q_ref, k_ref, v_ref, clip_ref, out_ref,
    qb, kb, vb, kl, vl, qa, far, far_lse, part, part_lse, hpart, hlse, extra, oin, oout, lin, lout, cw,
    load_sem, clip_sem, sib_send, sib_recv, left_send, left_recv, rest_send, rest_recv,
    q_send, q_recv, o_send, o_recv, l_send, l_recv, out_sem, out_send, out_recv,
):
    size = lax.axis_size("ctx")
    chips = size // 2
    me = lax.axis_index("ctx")
    core = lax.rem(me, 2)
    chip = me // 2
    sib = chip * 2 + (1 - core)
    prev = lax.rem(me + size - 2, size)
    nxt = lax.rem(me + 2, size)
    prev_sib = prev + 1 - 2 * core
    nxt_sib = nxt + 1 - 2 * core

    def remote(src, dst, send, recv, to):
        return pltpu.make_async_remote_copy(
            src_ref=src, dst_ref=dst, send_sem=send, recv_sem=recv,
            device_id={"ctx": to}, device_id_type=MESH,
        )

    mine = pl.ds(pl.multiple_of(core * HALF, HALF), HALF)
    theirs = pl.ds(pl.multiple_of((1 - core) * HALF, HALF), HALF)
    whole = pl.ds(0, HALF)
    front = pl.ds(0, HEAD_DIM)

    def moves(base):
        pairs = [(q_ref.at[whole, pl.ds(pl.multiple_of(base, HALF), HALF)], qb.at[0, mine])]
        for src, dst in ((k_ref, kb), (v_ref, vb)):
            for h in range(LANE_HEADS):
                cols = pl.ds(pl.multiple_of(base + h * HEAD_DIM, HEAD_DIM), HEAD_DIM)
                pairs.append((src.at[whole, cols], dst.at[h, mine, front]))
        return pairs

    loads = [
        pltpu.make_async_copy(src, dst, load_sem.at[i])
        for i, (src, dst) in enumerate(moves(core * HALF))
    ]
    for copy in loads:
        copy.start()
    clips = []
    for i in range(HOPS + 2):
        row = pl.multiple_of(lax.rem(chip + chips - 1 + i, chips) * 8, 8)
        clips.append(
            pltpu.make_async_copy(clip_ref.at[pl.ds(row, 8)], cw.at[pl.ds(8 * i, 8)], clip_sem.at[i])
        )
    for copy in clips:
        copy.start()
    lin[...] = jnp.zeros(lin.shape, F32)

    barrier = pltpu.get_barrier_semaphore()
    for to in (sib, prev, nxt, prev_sib, nxt_sib):
        pl.semaphore_signal(barrier, inc=1, device_id={"ctx": to}, device_id_type=MESH)

    for copy in clips:
        copy.wait()
    lane = lax.broadcasted_iota(jnp.int32, (128, 128), 1)

    def clip_columns(row):
        wide = jnp.broadcast_to(cw[pl.ds(row, 1), :].astype(F32), (128, 128))
        return wide.T.astype(jnp.int32)

    ones = jnp.ones((128, HEAD_DIM), BF16)

    def prepare_own():
        @pl.loop(0, 8)
        def _(i):
            same = clip_columns(8 + i) == lane
            r = pl.ds(pl.multiple_of(i * 128, 128), 128)
            mask = jnp.where(same | (lane >= 32), 0.0, -PENALTY).astype(BF16)
            for h in range(LANE_HEADS):
                kb[h, r, HEAD_DIM:] = mask
                vb[h, r, HEAD_DIM:] = ones
            qa[0, r, :] = jnp.where(same, 1.0, 0.0).astype(BF16)

    def prepare_left():
        @pl.loop(0, 4)
        def _(i):
            same = clip_columns(4 + i) == lane
            r = pl.ds(pl.multiple_of(i * 128, 128), 128)
            mask = jnp.where(same | (lane >= 32), 0.0, -PENALTY).astype(BF16)
            for h in range(LANE_HEADS):
                kl[h, r, HEAD_DIM:] = mask
                vl[h, r, HEAD_DIM:] = ones

    def prepare_visitors(start):
        @pl.loop(0, 12)
        def _(i):
            i = start + i
            same = clip_columns(16 + i) == lane
            r = pl.ds(pl.multiple_of(lax.rem(i, 8) * 128, 128), 128)
            qa[1 + i // 8, r, :] = jnp.where(same, 1.0, 0.0).astype(BF16)

    prepare_own()
    prepare_visitors(0)
    prepare_visitors(12)
    prepare_left()
    pl.semaphore_wait(barrier, 5)

    swaps = [
        remote(src, dst, sib_send.at[i], sib_recv.at[i], sib)
        for i, (src, dst) in enumerate(moves((1 - core) * HALF))
    ]

    def rows_of(k):
        block = jnp.where(k < K // 2, k + K // 2, K - 1 - k)
        return pl.ds(pl.multiple_of(block * T, T), T)

    def device_rows(k):
        block = jnp.where(k < K // 2, k, K - 1 - k)
        return pl.ds(pl.multiple_of(block * T, T), T)

    def send_q(d, k):
        r = rows_of(k)
        return remote(qb.at[d - 1, r], qb.at[d, r], q_send.at[d - 1], q_recv.at[d - 1, k], prev)

    def send_own(k, lane, to):
        cols = pl.ds(lane * WIDTH, WIDTH)
        return remote(q_ref.at[device_rows(k), cols], qb.at[1, rows_of(k)], q_send.at[0], q_recv.at[0, k], to)

    def start_own(k):
        @pl.when(core == 1 - k // (K // 2))
        def _():
            for lane in range(2):
                send_own(k, lane, 2 * (prev // 2) + lane).start()

    def send_o(d, k):
        r = rows_of(k)
        return remote(oout.at[d, r], oin.at[d - 1, r], o_send.at[d - 1], o_recv.at[d - 1, k], nxt)

    def send_l(d, k):
        rows = pl.ds(0, LANE_HEADS)
        return remote(
            lout.at[d, k, rows], lin.at[d - 1, k, rows], l_send.at[d - 1], l_recv.at[d - 1, k], nxt
        )

    def left_copy(i, early):
        h = i // 2
        src, mem, dst = ((k_ref, kb, kl), (v_ref, vb, vl))[i % 2]
        if early:
            cols = pl.ds(pl.multiple_of(core * WIDTH + h * HEAD_DIM, HEAD_DIM), HEAD_DIM)
            part_of = src.at[pl.ds(REST, HALF - REST), cols]
        else:
            part_of = mem.at[h, pl.ds(HALF + REST, HALF - REST), front]
        return remote(
            part_of, dst.at[h, pl.ds(REST, HALF - REST), front], left_send.at[i], left_recv.at[i], nxt
        )

    def rest_copy(i):
        h = i // 2
        mem, dst = ((kb, kl), (vb, vl))[i % 2]
        return remote(
            mem.at[h, pl.ds(HALF, REST), front], dst.at[h, pl.ds(0, REST), front],
            rest_send.at[i], rest_recv.at[i], nxt,
        )

    start_own(0)
    start_own(1)

    @pl.when(core == 1)
    def _():
        for i in range(2 * LANE_HEADS):
            left_copy(i, True).start()

    for copy in swaps:
        copy.start()

    def wide_rows(d, rows, h):
        return jnp.concatenate([qb[d, rows, h * HEAD_DIM : (h + 1) * HEAD_DIM], qa[d, rows, :]], axis=1)

    def own_block(b):
        rows, seen = pl.ds(b * FRAME, FRAME), pl.ds(0, (b + 1) * FRAME)
        if b == 0:
            for load, swap in zip(loads, swaps):
                load.wait()
                swap.wait_recv()

            @pl.when(core == 0)
            def _():
                for i in range(2 * LANE_HEADS):
                    left_copy(i, False).start()

        def store(h, value):
            hpart[rows, h * HEAD_DIM : (h + 1) * HEAD_DIM] = value

        hlse[rows, :] = attend(lambda h: wide_rows(0, rows, h), lambda h: kb[h, seen, :], lambda h: vb[h, seen, :], store)

    def hand_on(d, k, mixed, lse):
        oout[d, rows_of(k), :] = mixed.astype(BF16)
        if d > 0:
            send_o(d, k).start()
            lout[d, k] = lse.T[:8, :]
            send_l(d, k).start()

    def piece_out(k):
        return oout.at[0, rows_of(k)], out_ref.at[device_rows(k), mine]

    def give_local(k):
        src, dst = piece_out(k)
        return pltpu.make_async_copy(src, dst, out_sem.at[lax.rem(k, K // 2)])

    def give_remote(k):
        src, dst = piece_out(k)
        i = lax.rem(k, K // 2)
        return remote(src, dst, out_send.at[i], out_recv.at[i], sib)

    def relay(hop, k):
        send_q(hop, k).wait_recv()
        send_q(hop + 1, k).start()

    def farthest(k):
        r = rows_of(k)
        send_q(HOPS, k).wait_recv()

        def store(h, value):
            far[:, h * HEAD_DIM : (h + 1) * HEAD_DIM] = value

        far_lse[...] = attend(
            lambda h: wide_rows(HOPS, r, h), lambda h: kb[h], lambda h: vb[h], store
        )

        @pl.when(k == K // 2)
        def _():
            for i in range(2 * LANE_HEADS):
                left_copy(i, False).wait_recv()

        @pl.when(k == K - 1)
        def _():
            for i in range(2 * LANE_HEADS):
                rest_copy(i).wait_recv()

        def reach(start):
            keys = pl.ds(start, HALF - start)

            def store(h, value):
                extra[:, h * HEAD_DIM : (h + 1) * HEAD_DIM] = value

            lse = attend(
                lambda h: wide_rows(HOPS, r, h), lambda h: kl[h, keys, :], lambda h: vl[h, keys, :], store
            )
            mixed, lse = join(far[...], far_lse[...], extra[...], lse)
            far[...] = mixed
            far_lse[...] = lse

        @pl.when((k >= K // 2) & (k < K - 1))
        def _():
            reach(REST)

        @pl.when(k == K - 1)
        def _():
            reach(0)

        hand_on(HOPS, k, far[...], far_lse[...])

    def nearer(i, k):
        r = rows_of(k)

        def store(h, value):
            part[i, :, h * HEAD_DIM : (h + 1) * HEAD_DIM] = value

        part_lse[i] = attend(
            lambda h: jnp.concatenate([wide_rows(d, r, h) for d in range(1, HOPS)], axis=0),
            lambda h: kb[h], lambda h: vb[h], store,
        )

    def join_piece(d, i, k):
        r = rows_of(k)
        send_l(d + 1, k).wait_recv()
        send_o(d + 1, k).wait_recv()
        arrived = jnp.concatenate([lin[d, k], jnp.zeros((120, 128), F32)], axis=0).T[:T, :]
        if d == 0:
            mixed, lse = join(hpart[r, :], hlse[r, :], oin[d, r, :], arrived)
        else:
            here = slice((d - 1) * T, d * T)
            mixed, lse = join(part[i, here, :], part_lse[i, here, :], oin[d, r, :], arrived)
        hand_on(d, k, mixed, lse)
        if d == 0:
            for owner in range(2):
                @pl.when((k // (K // 2) == 1 - owner) & (core == owner))
                def _():
                    give_local(k).start()

                @pl.when((k // (K // 2) == 1 - owner) & (core != owner))
                def _():
                    give_remote(k).start()

    def all_sent():
        for copy in swaps:
            copy.wait_send()

        for i in range(2 * LANE_HEADS):
            left_copy(i, False).wait_send()
            rest_copy(i).wait_send()

        for d in range(1, HOPS + 1):
            remote(qb.at[d - 1], qb.at[d], q_send.at[d - 1], q_recv.at[d - 1, 0], prev).wait_send()
            remote(oout.at[d], oin.at[d - 1], o_send.at[d - 1], o_recv.at[d - 1, 0], nxt).wait_send()
            rows = pl.ds(0, LANE_HEADS)
            remote(
                lout.at[d, :, rows], lin.at[d - 1, :, rows], l_send.at[d - 1], l_recv.at[d - 1, 0], nxt
            ).wait_send()

    @pl.loop(0, K // 2 + 2)
    def _(p):
        hopping = p < K // 2
        coming = (p >= 1) & (p < K // 2 + 1)
        home = p >= 2

        def at(cond, *steps):
            @pl.when(cond)
            def _():
                for step in steps:
                    step()

        k, before, last = 2 * p, 2 * (p - 1), 2 * (p - 2)
        at(coming, lambda: farthest(before))
        at(coming, lambda: farthest(before + 1))
        at(hopping, lambda: relay(1, k))
        at(p == 0, lambda: own_block(0))
        at(coming, lambda: nearer(0, before), lambda: join_piece(2, 0, before))
        at(p == 1, *[rest_copy(i).start for i in range(0, 1)])
        at(p == 2, *[rest_copy(i).start for i in range(4, 5)])
        at(hopping, lambda: relay(1, k + 1))
        at(p == 0, lambda: own_block(1))
        at(hopping, lambda: relay(2, k))
        at(coming, lambda: nearer(1, before + 1), lambda: join_piece(2, 1, before + 1))
        at(p == 1, *[rest_copy(i).start for i in range(1, 2)])
        at(p == 2, *[rest_copy(i).start for i in range(5, 6)])
        at(p == 0, lambda: own_block(2))
        at(home, lambda: join_piece(0, 0, last))
        at(p == K // 2 + 1, all_sent)
        at(coming, lambda: join_piece(1, 0, before))
        at(p == 1, *[rest_copy(i).start for i in range(2, 3)])
        at(p == 2, *[rest_copy(i).start for i in range(6, 7)])
        at(hopping, lambda: relay(2, k + 1))
        at(p < K // 2 - 1, lambda: start_own(k + 2))
        at(p < K // 2 - 1, lambda: start_own(k + 3))
        at(p == 0, lambda: own_block(3))
        at(home, lambda: join_piece(0, 1, last + 1))
        at(coming, lambda: join_piece(1, 1, before + 1))
        at(p == 1, *[rest_copy(i).start for i in range(3, 4)])
        at(p == 2, *[rest_copy(i).start for i in range(7, 8)])

    @pl.loop(0, K // 2)
    def _(k):
        give_local(k).wait()
        give_remote(k).wait()


PLACES = 4


def place(src, dst, held, sem_in, sem_out):
    rows = src.shape[0] // PLACES
    spans = [pl.ds(i * rows, rows) for i in range(PLACES)]
    ins = [pltpu.make_async_copy(src.at[r], held.at[r], sem_in.at[i]) for i, r in enumerate(spans)]
    outs = [pltpu.make_async_copy(held.at[r], dst.at[r], sem_out.at[i]) for i, r in enumerate(spans)]
    for copy in ins:
        copy.start()
    for first, second in zip(ins, outs):
        first.wait()
        second.start()
    for copy in outs:
        copy.wait()


def per_device(queries, keys, values, clip_ids):
    tokens, width = queries.shape
    anywhere = pl.BlockSpec(memory_space=pl.ANY)
    dma = pltpu.SemaphoreType.DMA
    stacked = (HOPS - 1) * T
    moved = 1 + 2 * LANE_HEADS
    joined = pl.pallas_call(
        kernel,
        out_shape=jax.ShapeDtypeStruct((tokens, width), BF16),
        in_specs=[anywhere] * 4,
        out_specs=anywhere,
        scratch_shapes=[
            pltpu.VMEM((HOPS + 1, CHIP, WIDTH), BF16),
            pltpu.VMEM((LANE_HEADS, CHIP, 2 * HEAD_DIM), BF16),
            pltpu.VMEM((LANE_HEADS, CHIP, 2 * HEAD_DIM), BF16),
            pltpu.VMEM((LANE_HEADS, HALF, 2 * HEAD_DIM), BF16),
            pltpu.VMEM((LANE_HEADS, HALF, 2 * HEAD_DIM), BF16),
            pltpu.VMEM((HOPS + 1, CHIP, 128), BF16),
            pltpu.VMEM((T, WIDTH), F32),
            pltpu.VMEM((T, 128), F32),
            pltpu.VMEM((2, stacked, WIDTH), F32),
            pltpu.VMEM((2, stacked, 128), F32),
            pltpu.VMEM((CHIP, WIDTH), F32),
            pltpu.VMEM((CHIP, 128), F32),
            pltpu.VMEM((T, WIDTH), F32),
            pltpu.VMEM((HOPS, CHIP, WIDTH), BF16),
            pltpu.VMEM((HOPS + 1, CHIP, WIDTH), BF16),
            pltpu.VMEM((HOPS, K, 8, 128), F32),
            pltpu.VMEM((HOPS + 1, K, 8, 128), F32),
            pltpu.VMEM((8 * (HOPS + 2), 128), jnp.int32),
            dma((moved,)), dma((HOPS + 2,)), dma((moved,)), dma((moved,)),
            dma((moved - 1,)), dma((moved - 1,)), dma((moved - 1,)), dma((moved - 1,)),
            dma((HOPS,)), dma((HOPS, K)), dma((HOPS,)), dma((HOPS, K)), dma((HOPS,)), dma((HOPS, K)),
            dma((K // 2,)), dma((K // 2,)), dma((K // 2,)),
        ],
        compiler_params=pltpu.CompilerParams(
            collective_id=0, has_side_effects=True, vmem_limit_bytes=62 << 20
        ),
        name="chain_attention",
    )(queries, keys, values, clip_ids.reshape(-1, 128))
    return pl.pallas_call(
        place,
        out_shape=jax.ShapeDtypeStruct((tokens, width), BF16),
        in_specs=[anywhere],
        out_specs=anywhere,
        scratch_shapes=[pltpu.VMEM((tokens, width), BF16), dma((PLACES,)), dma((PLACES,))],
        name="place_result",
    )(joined)


def solution(mesh):
    placed = (P(("dp", "ctx"), None), P(("dp", "ctx"), None), P(("dp", "ctx"), None), P("dp"))
    return jax.shard_map(
        per_device, mesh=mesh, in_specs=placed, out_specs=P(("dp", "ctx"), None), check_vma=False
    )
```
